32 devices in a mesh: slab: 32 (over z, y, x, core).
Axes of the slice: x: 2, y: 2, z: 4, core: 2. Of those that a mesh axis runs over, the one named last changes fastest.
Arguments:
- velocity: float32 [3, 256, 32, 128], P(None, 'slab'), may hold values from -6 to 6
- node_coords: float32 [4096, 3, 128], P('slab'), may hold values from 0 to 1
- node_force: float32 [4096, 3, 128], P('slab'), may hold values from -12 to 12
- block_slab: int32 [4096, 1], P('slab'), may hold values from 0 to 31; in each aligned block of 128 rows (0 to 127, 128 to 255, ...) at most 8 rows name the same one
- block_offset: int32 [4096, 2], P('slab'), may hold values from 1 to 25
Outputs:
- new_velocity: float32 [3, 256, 32, 128], P(None, 'slab')
- node_velocity: float32 [4096, 3, 128], P('slab')
The draws below stay inside these ranges and needn't reach their ends.
Inputs may be any that keep to these rules, and one draw needn't show every extreme that they name: `block_slab`: among the 128 blocks of one device at most 8 name the same slab, and in every draw some device has exactly 8 blocks in one slab.
All inputs are finite; a program needn't handle non-finite values.
Results may differ from the reference program's by a relative error of at most 0.0003.
Values sent between devices are 32-bit elements; how exact they have to be, the bound alone decides.
A program may use at most 128 MiB of HBM per device.

```python
import math
import jax
import jax.numpy as jnp
import numpy as np
from jax import lax

CX = 8
NY = 32
NZ = 128
BS = 128
BLK_DEV = 128
SUBSTEPS = 3
CAP = 8
NX = 256
BLOCKS = 4096
N_SLAB = 32


def plant(values, own_key, low, largest):
    index_at = [jax.random.randint(jax.random.fold_in(own_key, axis), (), 0, length) for axis, length in enumerate(values.shape)]
    longest = values.shape.index(max(values.shape))
    neighbour = index_at[:longest] + [(index_at[longest] + 1) % values.shape[longest]] + index_at[longest + 1:]
    return values.at[tuple(index_at)].set(low).at[tuple(neighbour)].set(largest)


def steps_of(own_key, shape, cuts, low, high):
    loudness = 1.0
    for axis_at, blocks in cuts:
        heights = jax.random.uniform(jax.random.fold_in(jax.random.fold_in(own_key, 6), axis_at), (blocks,), jnp.float32, low / len(cuts), high / len(cuts))
        loudness = loudness * jnp.repeat(jnp.exp(heights), shape[axis_at] // blocks).reshape((-1,) + (1,) * (len(shape) - 1 - axis_at))
    return loudness


def deal_out(rng, own, number, rows, amount, top, bound, slope):
    sequence = jax.random.permutation(rng, amount)
    crowded, usual = load_shares(amount, rows * top, bound, slope, True), load_shares(amount, rows * top, bound, slope, False)
    places = jnp.arange(amount)

    def named(sizes, offset_by):
        used = int((sizes > 0).sum())
        fixed = max(1, used // 4)
        passed = fixed + (places - fixed + offset_by * (used - fixed)) % max(1, amount - fixed)
        return jnp.zeros((amount,), jnp.int32).at[sequence[jnp.where(places < fixed, places, passed)]].set(jnp.asarray(sizes, jnp.int32))

    sizes = jnp.where(number % 4 == 0, named(crowded, number // 4), named(usual, number - number // 4 - 1))
    mixed = jax.random.permutation(jax.random.fold_in(own, 3), amount)
    giver, sink = mixed[0:amount // 2 * 2:2], mixed[1:amount // 2 * 2:2]
    slack = jnp.minimum(sizes[giver] - 1, bound - sizes[sink]) // 2
    slack = jnp.where((giver == sequence[0]) | (sink == sequence[0]) | (sizes[sink] == 0), 0, jnp.maximum(slack, 0))
    passed = jax.random.randint(jax.random.fold_in(own, 4), (amount // 2,), 0, 1 << 20) % (slack + 1)
    sizes = sizes.at[giver].add(-passed).at[sink].add(passed)
    items = jnp.searchsorted(jnp.cumsum(sizes), jnp.arange(rows * top), side="right").astype(jnp.int32)
    grid = items.reshape(top, rows).T
    grid = grid[jax.random.permutation(jax.random.fold_in(own, 1), rows)]
    offset_by = jax.random.randint(jax.random.fold_in(own, 2), (rows, 1), 0, top)
    return jnp.take_along_axis(grid, (jnp.arange(top)[None, :] + offset_by) % top, axis=1)


def load_shares(amount, total, reach, slope, full):
    weights = [(1 << 20) // math.isqrt(standing ** slope) + 1 for standing in range(1, amount + 1)]
    largest = reach if full else min(reach, max(-(-total // amount), total * weights[0] // sum(weights)))
    least = 1 if total - largest >= amount - 1 else 0
    holding, spare = [largest] + [least] * (amount - 1), total - largest - least * (amount - 1)
    while spare > 0:
        candidates = [i for i in range(1, amount) if holding[i] < largest] or [i for i in range(1, amount) if holding[i] < reach]
        whole, remaining = sum([weights[i] for i in candidates]), spare
        for i in candidates:
            addition = min(reach - holding[i], max(1, remaining * weights[i] // whole), spare)
            holding[i] = holding[i] + addition
            spare = spare - addition
    return np.array(holding)


def bell_draw(rng, extent, deviation, limit, cuts=(), held_as=jnp.bfloat16):
    level = steps_of(rng, extent, cuts, -0.22, 0.18) if cuts else 1.0
    values = jax.random.normal(rng, extent, jnp.float32) * deviation * level
    return jnp.minimum(jnp.maximum(values, -limit), limit).astype(held_as)


def setup_inputs(seed: int = 0) -> dict:
    arg_keys = jax.random.split(jax.random.key(seed), 6)
    velocity = bell_draw(arg_keys[0], (3, NX, NY, NZ), 1.0, 6.0, ((1, 32),), jnp.float32)
    node_coords = jnp.clip(1.0 * jax.random.uniform(arg_keys[1], (BLOCKS, 3, BS), jnp.float32) ** steps_of(arg_keys[1], (BLOCKS, 3, BS), ((0, 32),), -0.2, 0.2), 0.0, 1.0)
    node_force = bell_draw(arg_keys[2], (BLOCKS, 3, BS), 2.0, 12.0, ((0, 32),), jnp.float32)
    block_slab_keys = jax.random.split(jax.random.fold_in(arg_keys[3], 1), BLOCKS // BLK_DEV)
    block_slab_turns = jax.random.permutation(jax.random.fold_in(arg_keys[3], 3), BLOCKS // BLK_DEV)
    block_slab = jax.vmap(lambda own, number: deal_out(jax.random.fold_in(arg_keys[3], 2), own, number, BLK_DEV, N_SLAB, 1, CAP, 2))(block_slab_keys, block_slab_turns).reshape((BLOCKS, 1))
    block_offset = plant(jax.random.randint(arg_keys[4], (BLOCKS, 2), 1, min(NY, NZ) - 6), jax.random.fold_in(arg_keys[4], 1), 1, (min(NY, NZ) - 6) - 1).astype(jnp.int32)
    return {"velocity": velocity, "node_coords": node_coords, "node_force": node_force, "block_slab": block_slab, "block_offset": block_offset}


time_step = 0.1
viscosity = 0.2


def kernel(distance):
    return jnp.where(jnp.abs(distance) < 2.0, 0.25 * (1.0 + jnp.cos(0.5 * math.pi * distance)), 0.0)


def node_weights(coords):
    planes = jnp.arange(CX, dtype=jnp.float32)
    taps = jnp.arange(8, dtype=jnp.float32)
    weight_x = kernel(planes[None, None, :] - 1.0 - (CX - 4) * coords[:, 0, :, None])
    weight_y = kernel(taps[None, None, :] - 1.0 - 5.0 * coords[:, 1, :, None])
    weight_z = kernel(taps[None, None, :] - 1.0 - 5.0 * coords[:, 2, :, None])
    count = coords.shape[0]
    nodes = coords.shape[2]
    joint = (weight_x[:, :, :, None] * weight_y[:, :, None, :]).reshape(count, nodes, CX * 8)
    return joint, weight_z


def make_patches(coords, force):
    count = coords.shape[0]
    nodes = coords.shape[2]
    joint, weight_z = node_weights(coords)
    force_z = (jnp.transpose(force, (0, 2, 1))[:, :, :, None] * weight_z[:, :, None, :]).reshape(count, nodes, 24)
    summed = jnp.einsum("knm,knq->kmq", joint, force_z, precision=lax.Precision.HIGHEST)
    summed = jnp.transpose(summed.reshape(count, CX, 8, 3, 8), (0, 3, 1, 2, 4))
    return summed.reshape(count, 3 * CX * 64)


def interpolate(flat, coords):
    count = coords.shape[0]
    joint, weight_z = node_weights(coords)
    values = flat.reshape(count, 3, CX * 8, 8)
    partial_sum = jnp.einsum("knm,kcmj->kncj", joint, values, precision=lax.Precision.HIGHEST)
    result = jnp.sum(partial_sum * weight_z[:, :, None, :], axis=3)
    return jnp.transpose(result, (0, 2, 1))


def grouped(function, arrays):
    count = arrays[0].shape[0]
    group = min(count, 128)
    shaped = tuple(a.reshape((count // group, group) + a.shape[1:]) for a in arrays)
    result = lax.map(lambda pieces: function(*pieces), shaped)
    return result.reshape((count,) + result.shape[2:])


def fluid_step(padded, forcing):
    center = padded[:, 1:-1]
    ahead = padded[:, 2:]
    behind = padded[:, :-2]
    y_plus = jnp.roll(center, -1, 2)
    y_minus = jnp.roll(center, 1, 2)
    z_plus = jnp.roll(center, -1, 3)
    z_minus = jnp.roll(center, 1, 3)
    laplace = ahead + behind + y_plus + y_minus + z_plus + z_minus - 6.0 * center
    advect = center[0:1] * (ahead - behind) * 0.5 + center[1:2] * (y_plus - y_minus) * 0.5 + center[2:3] * (z_plus - z_minus) * 0.5
    return center + time_step * (viscosity * laplace - advect + forcing)


def reference(velocity, node_coords, node_force, block_slab, block_offset):
    count = node_coords.shape[0]
    patches = grouped(make_patches, (node_coords, node_force)).reshape(count, 3, CX, 8, 8)
    taps = jnp.arange(8, dtype=jnp.int32)
    plane_index = block_slab[:, 0:1].astype(jnp.int32) * CX + jnp.arange(CX, dtype=jnp.int32)[None, :]
    row_index = block_offset[:, 0:1].astype(jnp.int32) - 1 + taps[None, :]
    col_index = block_offset[:, 1:2].astype(jnp.int32) - 1 + taps[None, :]
    index_x = plane_index[:, :, None, None]
    index_y = row_index[:, None, :, None]
    index_z = col_index[:, None, None, :]
    force_grid = jnp.zeros_like(velocity).at[:, index_x, index_y, index_z].add(jnp.transpose(patches, (1, 0, 2, 3, 4)))
    field = velocity
    for substep in range(SUBSTEPS):
        padded = jnp.concatenate([field[:, -1:], field, field[:, :1]], axis=1)
        field = fluid_step(padded, force_grid)
    beside_all = jnp.transpose(field[:, index_x, index_y, index_z], (1, 0, 2, 3, 4)).reshape(count, 3 * CX * 64)
    node_velocity = grouped(interpolate, (beside_all, node_coords))
    return field, node_velocity
```

```python
import functools

import jax
import jax.numpy as jnp
from jax import lax
from jax.experimental import pallas as pl
from jax.experimental.pallas import tpu as pltpu
from jax.sharding import PartitionSpec as P

CX = 8
SUBSTEPS = 3
TAPS = 8
NZF = 32
ROWS = 7
time_step = 0.1
viscosity = 0.2
COEF = (0.138840092, 0.00867750575, 0.000192567891, 2.21000608e-06, 1.5527319e-08, 7.70041313e-11)


def phi(r):
    u = jnp.maximum(4.0 - r * r, 0.0)
    q = jnp.full_like(u, COEF[-1])
    for c in COEF[-2::-1]:
        q = q * u + c
    q = q * u
    return q * q


def split(x):
    high = x.astype(jnp.bfloat16)
    return high, (x - high.astype(jnp.float32)).astype(jnp.bfloat16)


def joint_weights(rec, s, r, cap, start, iota8):
    cx = rec[s, r:r + 1, :]
    cy = rec[s, cap + r:cap + r + 1, :]
    first = rec[s, 6 * cap + r:6 * cap + r + 1, 0:1]
    wx = phi(iota8 - 1.0 - (CX - 4) * cx)
    wy = phi(iota8 + (start.astype(jnp.float32) - first) - 5.0 * cy)
    return (wy[:, None, :] * wx[None, :, :]).reshape(TAPS * CX, cx.shape[-1])


def z_weights(rec, s, r, cap, iota32):
    cz = rec[s, 2 * cap + r:2 * cap + r + 1, :]
    first = rec[s, 6 * cap + r:6 * cap + r + 1, 1:2]
    return phi(iota32 - first - 5.0 * cz)


def window_start(starts, slot, ny):
    return jnp.clip(starts[slot] - 1, 0, ny - TAPS)


def pack_kernel(cap, slab, offset, coords, force, send, slots, count):
    devices = send.shape[0]
    send[...] = jnp.zeros_like(send)

    def clear(d, carry):
        count[d] = 0
        return carry

    lax.fori_loop(0, devices, clear, 0)
    lane = lax.broadcasted_iota(jnp.int32, (1, send.shape[2]), 1)

    def one(k, carry):
        d = slab[k]
        r = count[d]
        count[d] = r + 1
        slots[k] = d * cap + r
        for c in range(3):
            send[d, pl.ds(c * cap + r, 1), :] = coords[k, c:c + 1, :]
            send[d, pl.ds((3 + c) * cap + r, 1), :] = force[k, c:c + 1, :]
        oy = offset[2 * k].astype(jnp.float32)
        oz = offset[2 * k + 1].astype(jnp.float32)
        send[d, pl.ds(6 * cap + r, 1), :] = jnp.where(lane == 0, oy, oz)
        return carry

    lax.fori_loop(0, coords.shape[0], one, 0, unroll=4)


def spread_kernel(cap, ny, starts, rec, out, acc):
    nodes = rec.shape[2]
    acc[...] = jnp.zeros_like(acc)
    iota8 = lax.broadcasted_iota(jnp.int32, (TAPS, nodes), 0).astype(jnp.float32)
    iota32 = lax.broadcasted_iota(jnp.int32, (NZF, nodes), 0).astype(jnp.float32)

    def source(s, carry):
        for r in range(cap):
            start = window_start(starts, s * cap + r, ny)
            joint = joint_weights(rec, s, r, cap, start, iota8)
            wz = z_weights(rec, s, r, cap, iota32)
            fz = jnp.concatenate(
                [rec[s, (3 + c) * cap + r:(3 + c) * cap + r + 1, :] * wz for c in range(3)], axis=0
            )
            jh, jl = split(joint)
            fh, fl = split(fz)
            patch = lax.dot_general(
                jnp.concatenate([jh, jl, jh], axis=1),
                jnp.concatenate([fh, fh, fl], axis=1),
                (((1,), (1,)), ((), ())),
                preferred_element_type=jnp.float32,
            )
            rows = pl.ds(pl.multiple_of(start * CX, CX), TAPS * CX)
            acc[rows, 0:3 * NZF] += patch
        return carry

    lax.fori_loop(0, rec.shape[0], source, 0)
    for a in range(CX):
        out[a] = acc[pl.ds(a, ny, stride=CX), :]


def fluid_kernel(cap, starts, vel, vleft, vright, fmid, fleft, fright, rec, new, back, u0, u1, fext, u4):
    planes, ny, nz = vel.shape[1], vel.shape[2], vel.shape[3]
    nodes = rec.shape[2]
    u0[:, 0:3] = vleft[...]
    u0[:, 3:3 + planes] = vel[...]
    u0[:, 3 + planes:6 + planes] = vright[...]
    fext[0:2] = fleft[...]
    fext[2:2 + planes] = fmid[...]
    fext[2 + planes:4 + planes] = fright[...]
    lane = lax.broadcasted_iota(jnp.int32, (ny, nz), 1)

    def step(src, dst, first, last):
        def plane(p, carry):
            packed = fext[p - 1]
            center = [src[c, p] for c in range(3)]
            for c in range(3):
                mid = center[c]
                ahead = src[c, p + 1]
                behind = src[c, p - 1]
                y_plus = pltpu.roll(mid, ny - 1, 0)
                y_minus = pltpu.roll(mid, 1, 0)
                z_plus = pltpu.roll(mid, nz - 1, 1)
                z_minus = pltpu.roll(mid, 1, 1)
                push = packed if c == 0 else pltpu.roll(packed, nz - c * NZF, 1)
                push = jnp.where(lane < NZF, push, 0.0)
                laplace = ahead + behind + y_plus + y_minus + z_plus + z_minus - 6.0 * mid
                advect = (
                    center[0] * (ahead - behind)
                    + center[1] * (y_plus - y_minus)
                    + center[2] * (z_plus - z_minus)
                ) * 0.5
                dst[c, p] = mid + time_step * (viscosity * laplace - advect + push)
            return carry

        lax.fori_loop(first, last, plane, 0)

    step(u0, u1, 1, planes + 5)
    step(u1, u0, 2, planes + 4)
    step(u0, u1, 3, planes + 3)
    new[...] = u1[:, 3:3 + planes]

    def gather(a, carry):
        for c in range(3):
            u = u1[c, 3 + a][:, 0:NZF]
            high = u.astype(jnp.bfloat16).astype(jnp.float32)
            low = u - high
            u4[c, pl.ds(a, ny, stride=CX), :] = jnp.concatenate([high, low, high, low], axis=1)
        return carry

    for a in range(CX):
        gather(a, 0)

    iota8 = lax.broadcasted_iota(jnp.int32, (TAPS, nodes), 0).astype(jnp.float32)
    iota32 = lax.broadcasted_iota(jnp.int32, (NZF, nodes), 0).astype(jnp.float32)

    def source(s, carry):
        for r in range(cap):
            start = window_start(starts, s * cap + r, ny)
            joint = joint_weights(rec, s, r, cap, start, iota8)
            wh, wl = split(z_weights(rec, s, r, cap, iota32))
            rows = pl.ds(pl.multiple_of(start * CX, CX), TAPS * CX)
            window = jnp.concatenate([u4[c, rows, :] for c in range(3)], axis=0).astype(jnp.bfloat16)
            part = jnp.dot(
                window, jnp.concatenate([wh, wh, wl, wl], axis=0), preferred_element_type=jnp.float32
            )
            for c in range(3):
                mine = part[c * TAPS * CX:(c + 1) * TAPS * CX] * joint
                back[s, c * cap + r:c * cap + r + 1, :] = jnp.sum(mine, axis=0, keepdims=True)
        return carry

    lax.fori_loop(0, rec.shape[0], source, 0)


def unpack_kernel(cap, slots, got, out):
    def one(k, carry):
        slot = slots[k]
        d = slot // cap
        r = slot - d * cap
        for c in range(3):
            out[k, c:c + 1, :] = got[d, pl.ds(c * cap + r, 1), :]
        return carry

    lax.fori_loop(0, out.shape[0], one, 0, unroll=4)


VMEM = pl.BlockSpec(memory_space=pltpu.VMEM)
SMEM = pl.BlockSpec(memory_space=pltpu.SMEM)
PARAMS = pltpu.CompilerParams(vmem_limit_bytes=40 * 1024 * 1024)


def body(velocity, node_coords, node_force, block_slab, block_offset):
    devices = lax.axis_size("slab")
    blocks, _, nodes = node_coords.shape
    cap = 2 * blocks // devices
    _, planes, ny, nz = velocity.shape
    f32 = jnp.float32

    up = [(i, (i + 1) % devices) for i in range(devices)]
    down = [((i + 1) % devices, i) for i in range(devices)]
    vleft = lax.ppermute(velocity[:, planes - 3:], "slab", up)
    vright = lax.ppermute(velocity[:, :3], "slab", down)

    send, slots = pl.pallas_call(
        functools.partial(pack_kernel, cap),
        out_shape=(
            jax.ShapeDtypeStruct((devices, ROWS * cap, nodes), f32),
            jax.ShapeDtypeStruct((blocks,), jnp.int32),
        ),
        in_specs=[SMEM, SMEM, VMEM, VMEM],
        out_specs=(VMEM, SMEM),
        scratch_shapes=[pltpu.SMEM((devices,), jnp.int32)],
        compiler_params=PARAMS,
    )(block_slab.reshape(blocks), block_offset.reshape(2 * blocks), node_coords, node_force)

    rec = lax.all_to_all(send, "slab", split_axis=0, concat_axis=0, tiled=True)
    starts = rec[:, 6 * cap:, 0].astype(jnp.int32).reshape(devices * cap)

    fmid = pl.pallas_call(
        functools.partial(spread_kernel, cap, ny),
        out_shape=jax.ShapeDtypeStruct((planes, ny, nz), f32),
        in_specs=[SMEM, VMEM],
        out_specs=VMEM,
        scratch_shapes=[pltpu.VMEM((ny * CX, nz), f32)],
        compiler_params=PARAMS,
    )(starts, rec)

    fleft = lax.ppermute(fmid[planes - 2:], "slab", up)
    fright = lax.ppermute(fmid[:2], "slab", down)

    new, back = pl.pallas_call(
        functools.partial(fluid_kernel, cap),
        out_shape=(
            jax.ShapeDtypeStruct(velocity.shape, f32),
            jax.ShapeDtypeStruct((devices, 3 * cap, nodes), f32),
        ),
        in_specs=[SMEM] + [VMEM] * 7,
        out_specs=(VMEM, VMEM),
        scratch_shapes=[
            pltpu.VMEM((3, planes + 6, ny, nz), f32),
            pltpu.VMEM((3, planes + 6, ny, nz), f32),
            pltpu.VMEM((planes + 4, ny, nz), f32),
            pltpu.VMEM((3, ny * CX, nz), f32),
        ],
        compiler_params=PARAMS,
    )(starts, velocity, vleft, vright, fmid, fleft, fright, rec)

    got = lax.all_to_all(back, "slab", split_axis=0, concat_axis=0, tiled=True)

    node_velocity = pl.pallas_call(
        functools.partial(unpack_kernel, cap),
        out_shape=jax.ShapeDtypeStruct((blocks, 3, nodes), f32),
        in_specs=[SMEM, VMEM],
        out_specs=VMEM,
        compiler_params=PARAMS,
    )(slots, got)
    return new, node_velocity


def solution(mesh):
    return jax.shard_map(
        body,
        mesh=mesh,
        in_specs=(
            P(None, "slab", None, None),
            P("slab", None, None),
            P("slab", None, None),
            P("slab", None),
            P("slab", None),
        ),
        out_specs=(P(None, "slab", None, None), P("slab", None, None)),
        check_vma=False,
    )
```

```python
import functools

import jax
import jax.numpy as jnp
from jax import lax
from jax.experimental import pallas as pl
from jax.experimental.pallas import tpu as pltpu
from jax.sharding import PartitionSpec as P

CX = 8
SUBSTEPS = 3
TAPS = 8
NZF = 32
ROWS = 7
time_step = 0.1
viscosity = 0.2
COEF = (0.138840092, 0.00867750575, 0.000192567891, 2.21000608e-06, 1.5527319e-08, 7.70041313e-11)


def phi(r):
    u = jnp.maximum(4.0 - r * r, 0.0)
    q = jnp.full_like(u, COEF[-1])
    for c in COEF[-2::-1]:
        q = q * u + c
    q = q * u
    return q * q


def split(x):
    high = x.astype(jnp.bfloat16)
    return high, (x - high.astype(jnp.float32)).astype(jnp.bfloat16)


def joint_weights(rec, s, r, cap, start, iota8):
    cx = rec[s, r:r + 1, :]
    cy = rec[s, cap + r:cap + r + 1, :]
    first = rec[s, 6 * cap + r:6 * cap + r + 1, 0:1]
    wx = phi(iota8 - 1.0 - (CX - 4) * cx)
    wy = phi(iota8 + (start.astype(jnp.float32) - first) - 5.0 * cy)
    return (wy[:, None, :] * wx[None, :, :]).reshape(TAPS * CX, cx.shape[-1])


def z_weights(rec, s, r, cap, iota32):
    cz = rec[s, 2 * cap + r:2 * cap + r + 1, :]
    first = rec[s, 6 * cap + r:6 * cap + r + 1, 1:2]
    return phi(iota32 - first - 5.0 * cz)


def pack_kernel(cap, slab, offset, coords, force, send, slots, count):
    devices = send.shape[0]
    send[...] = jnp.zeros_like(send)

    def clear(d, carry):
        count[d] = 0
        return carry

    lax.fori_loop(0, devices, clear, 0)
    lane = lax.broadcasted_iota(jnp.int32, (1, send.shape[2]), 1)

    def one(k, carry):
        d = slab[k]
        r = count[d]
        count[d] = r + 1
        slots[k] = d * cap + r
        for c in range(3):
            send[d, pl.ds(c * cap + r, 1), :] = coords[k, c:c + 1, :]
            send[d, pl.ds((3 + c) * cap + r, 1), :] = force[k, c:c + 1, :]
        oy = offset[2 * k].astype(jnp.float32)
        oz = offset[2 * k + 1].astype(jnp.float32)
        send[d, pl.ds(6 * cap + r, 1), :] = jnp.where(lane == 0, oy, oz)
        return carry

    lax.fori_loop(0, coords.shape[0], one, 0, unroll=4)


def spread_kernel(cap, ny, starts, rec, out, acc):
    nodes = rec.shape[2]
    acc[...] = jnp.zeros_like(acc)
    iota8 = lax.broadcasted_iota(jnp.int32, (TAPS, nodes), 0).astype(jnp.float32)
    iota32 = lax.broadcasted_iota(jnp.int32, (NZF, nodes), 0).astype(jnp.float32)

    def source(s, carry):
        for r in range(cap):
            start = starts[s * cap + r]
            joint = joint_weights(rec, s, r, cap, start, iota8)
            wz = z_weights(rec, s, r, cap, iota32)
            fz = jnp.concatenate(
                [rec[s, (3 + c) * cap + r:(3 + c) * cap + r + 1, :] * wz for c in range(3)], axis=0
            )
            jh, jl = split(joint)
            fh, fl = split(fz)
            patch = lax.dot_general(
                jnp.concatenate([jh, jl, jh], axis=1),
                jnp.concatenate([fh, fh, fl], axis=1),
                (((1,), (1,)), ((), ())),
                preferred_element_type=jnp.float32,
            )
            rows = pl.ds(pl.multiple_of(start * CX, CX), TAPS * CX)
            acc[rows, 0:3 * NZF] += patch
        return carry

    lax.fori_loop(0, rec.shape[0], source, 0)
    for a in range(CX):
        out[a] = acc[pl.ds(a, ny, stride=CX), :]


def partner(j, n):
    half = (j + 1) // 2
    return n // 2 + half * (1 - 2 * (j % 2))


def meet_all(n, me):
    barrier = pltpu.get_barrier_semaphore()

    def greet(i, carry):
        pl.semaphore_signal(barrier, inc=1, device_id=(lax.rem(me + i, n),), device_id_type=MESH)
        return carry

    lax.fori_loop(1, n, greet, 0)
    pl.semaphore_wait(barrier, n - 1)


def exchange_kernel(n, send, vel, rec, vleft, vright, send_sem, recv_sem, own_sem, halo_send, halo_recv):
    me = lax.axis_index("slab")
    right, left = lax.rem(me + 1, n), lax.rem(me + n - 1, n)
    planes = vel.shape[1]
    own = pltpu.make_async_copy(send.at[me], rec.at[me], own_sem)
    own.start()
    meet_all(n, me)

    def copy_to(i):
        to = lax.rem(me + i, n)
        return pltpu.make_async_remote_copy(
            src_ref=send.at[to], dst_ref=rec.at[me], send_sem=send_sem.at[i], recv_sem=recv_sem.at[i],
            device_id=(to,), device_id_type=MESH,
        )

    halos = [
        pltpu.make_async_remote_copy(
            src_ref=vel.at[:, planes - 3:], dst_ref=vleft, send_sem=halo_send.at[0], recv_sem=halo_recv.at[0],
            device_id=(right,), device_id_type=MESH,
        ),
        pltpu.make_async_remote_copy(
            src_ref=vel.at[:, 0:3], dst_ref=vright, send_sem=halo_send.at[1], recv_sem=halo_recv.at[1],
            device_id=(left,), device_id_type=MESH,
        ),
    ]

    def start(j, carry):
        copy_to(partner(j, n)).start()
        return carry

    lax.fori_loop(0, n - 1, start, 0)
    for halo in halos:
        halo.start()

    def finish(i, carry):
        copy = pltpu.make_async_remote_copy(
            src_ref=send.at[lax.rem(me + i, n)], dst_ref=rec.at[lax.rem(me + n - i, n)],
            send_sem=send_sem.at[i], recv_sem=recv_sem.at[i], device_id=(right,), device_id_type=MESH,
        )
        copy.wait()
        return carry

    lax.fori_loop(1, n, finish, 0)
    for halo in halos:
        halo.wait()
    own.wait()


def fluid_kernel(
    n, cap, starts, vel, vleft, vright, fmid, rec, new, got,
    u0, u1, fext, u4, back, send_sem, recv_sem, halo_send, halo_recv,
):
    me = lax.axis_index("slab")
    right, left = lax.rem(me + 1, n), lax.rem(me + n - 1, n)
    planes, ny, nz = vel.shape[1], vel.shape[2], vel.shape[3]
    nodes = rec.shape[2]
    meet_all(n, me)
    halos = [
        pltpu.make_async_remote_copy(
            src_ref=fmid.at[planes - 2:], dst_ref=fext.at[0:2], send_sem=halo_send.at[0],
            recv_sem=halo_recv.at[0], device_id=(right,), device_id_type=MESH,
        ),
        pltpu.make_async_remote_copy(
            src_ref=fmid.at[0:2], dst_ref=fext.at[2 + planes:4 + planes], send_sem=halo_send.at[1],
            recv_sem=halo_recv.at[1], device_id=(left,), device_id_type=MESH,
        ),
    ]
    for halo in halos:
        halo.start()
    u0[:, 0:3] = vleft[...]
    u0[:, 3:3 + planes] = vel[...]
    u0[:, 3 + planes:6 + planes] = vright[...]
    lane = lax.broadcasted_iota(jnp.int32, (ny, nz), 1)

    def step(src, dst, first, last, force, shift):
        def plane(p, carry):
            packed = force[p - shift]
            center = [src[c, p] for c in range(3)]
            for c in range(3):
                mid = center[c]
                ahead = src[c, p + 1]
                behind = src[c, p - 1]
                y_plus = pltpu.roll(mid, ny - 1, 0)
                y_minus = pltpu.roll(mid, 1, 0)
                z_plus = pltpu.roll(mid, nz - 1, 1)
                z_minus = pltpu.roll(mid, 1, 1)
                push = packed if c == 0 else pltpu.roll(packed, nz - c * NZF, 1)
                push = jnp.where(lane < NZF, push, 0.0)
                laplace = ahead + behind + y_plus + y_minus + z_plus + z_minus - 6.0 * mid
                advect = (
                    center[0] * (ahead - behind)
                    + center[1] * (y_plus - y_minus)
                    + center[2] * (z_plus - z_minus)
                ) * 0.5
                dst[c, p] = mid + time_step * (viscosity * laplace - advect + push)
            return carry

        lax.fori_loop(first, last, plane, 0)

    step(u0, u1, 3, planes + 3, fmid, 3)
    for halo in halos:
        halo.wait()
    step(u0, u1, 1, 3, fext, 1)
    step(u0, u1, planes + 3, planes + 5, fext, 1)
    step(u1, u0, 2, 3, fext, 1)
    step(u1, u0, 3, planes + 3, fmid, 3)
    step(u1, u0, planes + 3, planes + 4, fext, 1)
    step(u0, u1, 3, planes + 3, fmid, 3)
    new[...] = u1[:, 3:3 + planes]

    for a in range(CX):
        for c in range(3):
            u = u1[c, 3 + a][:, 0:NZF]
            high = u.astype(jnp.bfloat16).astype(jnp.float32)
            low = u - high
            u4[c, :, a, :] = jnp.concatenate([high, low, high, low], axis=1)

    iota8 = lax.broadcasted_iota(jnp.int32, (TAPS, nodes), 0).astype(jnp.float32)
    iota32 = lax.broadcasted_iota(jnp.int32, (NZF, nodes), 0).astype(jnp.float32)

    def answer(s, put, place):
        for r in range(cap):
            start = starts[s * cap + r]
            joint = joint_weights(rec, s, r, cap, start, iota8)
            wh, wl = split(z_weights(rec, s, r, cap, iota32))
            window = jnp.concatenate(
                [u4[c, start + i] for c in range(3) for i in range(TAPS)], axis=0
            ).astype(jnp.bfloat16)
            part = jnp.dot(
                window, jnp.concatenate([wh, wh, wl, wl], axis=0), preferred_element_type=jnp.float32
            )
            for c in range(3):
                mine = part[c * TAPS * CX:(c + 1) * TAPS * CX] * joint
                put[place, c * cap + r:c * cap + r + 1, :] = jnp.sum(mine, axis=0, keepdims=True)

    def serve(j, carry):
        i = partner(j, n)
        s = lax.rem(me + i, n)
        answer(s, back, s)
        pltpu.make_async_remote_copy(
            src_ref=back.at[s], dst_ref=got.at[me], send_sem=send_sem.at[i], recv_sem=recv_sem.at[i],
            device_id=(s,), device_id_type=MESH,
        ).start()
        return carry

    lax.fori_loop(0, n - 1, serve, 0)
    answer(me, got, me)

    def finish(i, carry):
        pltpu.make_async_remote_copy(
            src_ref=back.at[lax.rem(me + i, n)], dst_ref=got.at[lax.rem(me + n - i, n)],
            send_sem=send_sem.at[i], recv_sem=recv_sem.at[i], device_id=(right,), device_id_type=MESH,
        ).wait()
        return carry

    lax.fori_loop(1, n, finish, 0)


def unpack_kernel(cap, slots, got, out):
    def one(k, carry):
        slot = slots[k]
        d = slot // cap
        r = slot - d * cap
        for c in range(3):
            out[k, c:c + 1, :] = got[d, pl.ds(c * cap + r, 1), :]
        return carry

    lax.fori_loop(0, out.shape[0], one, 0, unroll=4)


MESH = pl.DeviceIdType.MESH
VMEM = pl.BlockSpec(memory_space=pltpu.VMEM)
SMEM = pl.BlockSpec(memory_space=pltpu.SMEM)
PARAMS = pltpu.CompilerParams(vmem_limit_bytes=40 * 1024 * 1024)


def body(velocity, node_coords, node_force, block_slab, block_offset):
    devices = lax.axis_size("slab")
    blocks, _, nodes = node_coords.shape
    cap = 2 * blocks // devices
    _, planes, ny, nz = velocity.shape
    f32 = jnp.float32

    send, slots = pl.pallas_call(
        functools.partial(pack_kernel, cap),
        out_shape=(
            jax.ShapeDtypeStruct((devices, ROWS * cap, nodes), f32),
            jax.ShapeDtypeStruct((blocks,), jnp.int32),
        ),
        in_specs=[SMEM, SMEM, VMEM, VMEM],
        out_specs=(VMEM, SMEM),
        scratch_shapes=[pltpu.SMEM((devices,), jnp.int32)],
        compiler_params=PARAMS,
    )(block_slab.reshape(blocks), block_offset.reshape(2 * blocks), node_coords, node_force)

    halo = jax.ShapeDtypeStruct((3, 3, ny, nz), f32)
    rec, vleft, vright = pl.pallas_call(
        functools.partial(exchange_kernel, devices),
        out_shape=(jax.ShapeDtypeStruct(send.shape, f32), halo, halo),
        in_specs=[VMEM, VMEM],
        out_specs=(VMEM, VMEM, VMEM),
        scratch_shapes=[
            pltpu.SemaphoreType.DMA((devices,)),
            pltpu.SemaphoreType.DMA((devices,)),
            pltpu.SemaphoreType.DMA,
            pltpu.SemaphoreType.DMA((2,)),
            pltpu.SemaphoreType.DMA((2,)),
        ],
        compiler_params=pltpu.CompilerParams(
            vmem_limit_bytes=40 * 1024 * 1024, collective_id=0, has_side_effects=True
        ),
    )(send, velocity)
    first = rec[:, 6 * cap:, 0].astype(jnp.int32).reshape(devices * cap)
    starts = jnp.clip(first - 1, 0, ny - TAPS)

    fmid = pl.pallas_call(
        functools.partial(spread_kernel, cap, ny),
        out_shape=jax.ShapeDtypeStruct((planes, ny, nz), f32),
        in_specs=[SMEM, VMEM],
        out_specs=VMEM,
        scratch_shapes=[pltpu.VMEM((ny * CX, nz), f32)],
        compiler_params=PARAMS,
    )(starts, rec)

    new, got = pl.pallas_call(
        functools.partial(fluid_kernel, devices, cap),
        out_shape=(
            jax.ShapeDtypeStruct(velocity.shape, f32),
            jax.ShapeDtypeStruct((devices, 3 * cap, nodes), f32),
        ),
        in_specs=[SMEM] + [VMEM] * 5,
        out_specs=(VMEM, VMEM),
        scratch_shapes=[
            pltpu.VMEM((3, planes + 6, ny, nz), f32),
            pltpu.VMEM((3, planes + 6, ny, nz), f32),
            pltpu.VMEM((planes + 4, ny, nz), f32),
            pltpu.VMEM((3, ny, CX, nz), f32),
            pltpu.VMEM((devices, 3 * cap, nodes), f32),
            pltpu.SemaphoreType.DMA((devices,)),
            pltpu.SemaphoreType.DMA((devices,)),
            pltpu.SemaphoreType.DMA((2,)),
            pltpu.SemaphoreType.DMA((2,)),
        ],
        compiler_params=pltpu.CompilerParams(
            vmem_limit_bytes=40 * 1024 * 1024, collective_id=1, has_side_effects=True
        ),
    )(starts, velocity, vleft, vright, fmid, rec)

    node_velocity = pl.pallas_call(
        functools.partial(unpack_kernel, cap),
        out_shape=jax.ShapeDtypeStruct((blocks, 3, nodes), f32),
        in_specs=[SMEM, VMEM],
        out_specs=VMEM,
        compiler_params=PARAMS,
    )(slots, got)
    return new, node_velocity


def solution(mesh):
    return jax.shard_map(
        body,
        mesh=mesh,
        in_specs=(
            P(None, "slab", None, None),
            P("slab", None, None),
            P("slab", None, None),
            P("slab", None),
            P("slab", None),
        ),
        out_specs=(P(None, "slab", None, None), P("slab", None, None)),
        check_vma=False,
    )
```

```python
import functools

import jax
import jax.numpy as jnp
from jax import lax
from jax.experimental import pallas as pl
from jax.experimental.pallas import tpu as pltpu
from jax.sharding import PartitionSpec as P

CX = 8
SUBSTEPS = 3
TAPS = 8
NZF = 32
ROWS = 7
time_step = 0.1
viscosity = 0.2
COEF = (0.138840092, 0.00867750575, 0.000192567891, 2.21000608e-06, 1.5527319e-08, 7.70041313e-11)


def phi(r):
    u = jnp.maximum(4.0 - r * r, 0.0)
    q = jnp.full_like(u, COEF[-1])
    for c in COEF[-2::-1]:
        q = q * u + c
    q = q * u
    return q * q


def split(x):
    high = x.astype(jnp.bfloat16)
    return high, (x - high.astype(jnp.float32)).astype(jnp.bfloat16)


def joint_weights(rec, s, r, cap, start, iota8):
    cx = rec[s, r:r + 1, :]
    cy = rec[s, cap + r:cap + r + 1, :]
    first = rec[s, 6 * cap + r:6 * cap + r + 1, 0:1]
    wx = phi(iota8 - 1.0 - (CX - 4) * cx)
    wy = phi(iota8 + (start.astype(jnp.float32) - first) - 5.0 * cy)
    return (wy[:, None, :] * wx[None, :, :]).reshape(TAPS * CX, cx.shape[-1])


def z_weights(rec, s, r, cap, iota32):
    cz = rec[s, 2 * cap + r:2 * cap + r + 1, :]
    first = rec[s, 6 * cap + r:6 * cap + r + 1, 1:2]
    return phi(iota32 - first - 5.0 * cz)


def pack_kernel(cap, slab, offset, coords, force, send, slots, count):
    devices = send.shape[0]
    send[...] = jnp.zeros_like(send)

    def clear(d, carry):
        count[d] = 0
        return carry

    lax.fori_loop(0, devices, clear, 0)
    lane = lax.broadcasted_iota(jnp.int32, (1, send.shape[2]), 1)

    def one(k, carry):
        d = slab[k]
        r = count[d]
        count[d] = r + 1
        slots[k] = d * cap + r
        for c in range(3):
            send[d, pl.ds(c * cap + r, 1), :] = coords[c, pl.ds(k, 1), :]
            send[d, pl.ds((3 + c) * cap + r, 1), :] = force[c, pl.ds(k, 1), :]
        oy = offset[2 * k].astype(jnp.float32)
        oz = offset[2 * k + 1].astype(jnp.float32)
        send[d, pl.ds(6 * cap + r, 1), :] = jnp.where(lane == 0, oy, oz)
        return carry

    lax.fori_loop(0, coords.shape[1], one, 0, unroll=4)


def spread_kernel(cap, ny, starts, rec, out, acc):
    nodes = rec.shape[2]
    acc[...] = jnp.zeros_like(acc)
    iota8 = lax.broadcasted_iota(jnp.int32, (TAPS, nodes), 0).astype(jnp.float32)
    iota32 = lax.broadcasted_iota(jnp.int32, (NZF, nodes), 0).astype(jnp.float32)

    def source(s, carry):
        for r in range(cap):
            start = starts[s * cap + r]
            joint = joint_weights(rec, s, r, cap, start, iota8)
            wz = z_weights(rec, s, r, cap, iota32)
            fz = jnp.concatenate(
                [rec[s, (3 + c) * cap + r:(3 + c) * cap + r + 1, :] * wz for c in range(3)], axis=0
            )
            jh, jl = split(joint)
            fh, fl = split(fz)
            patch = lax.dot_general(
                jnp.concatenate([jh, jl, jh], axis=1),
                jnp.concatenate([fh, fh, fl], axis=1),
                (((1,), (1,)), ((), ())),
                preferred_element_type=jnp.float32,
            )
            rows = pl.ds(pl.multiple_of(start * CX, CX), TAPS * CX)
            acc[rows, 0:3 * NZF] += patch
        return carry

    lax.fori_loop(0, rec.shape[0], source, 0)
    for a in range(CX):
        out[a] = acc[pl.ds(a, ny, stride=CX), :]


def partner(j, n):
    half = (j + 1) // 2
    return n // 2 + half * (1 - 2 * (j % 2))


def meet_all(n, me):
    barrier = pltpu.get_barrier_semaphore()

    def greet(i, carry):
        pl.semaphore_signal(barrier, inc=1, device_id=(lax.rem(me + i, n),), device_id_type=MESH)
        return carry

    lax.fori_loop(1, n, greet, 0)
    pl.semaphore_wait(barrier, n - 1)


def exchange_kernel(n, send, vel, rec, vleft, vright, send_sem, recv_sem, own_sem, halo_send, halo_recv):
    me = lax.axis_index("slab")
    right, left = lax.rem(me + 1, n), lax.rem(me + n - 1, n)
    planes = vel.shape[1]
    own = pltpu.make_async_copy(send.at[me], rec.at[me], own_sem)
    own.start()
    meet_all(n, me)

    def copy_to(i):
        to = lax.rem(me + i, n)
        return pltpu.make_async_remote_copy(
            src_ref=send.at[to], dst_ref=rec.at[me], send_sem=send_sem.at[i], recv_sem=recv_sem.at[i],
            device_id=(to,), device_id_type=MESH,
        )

    halos = [
        pltpu.make_async_remote_copy(
            src_ref=vel.at[:, planes - 3:], dst_ref=vleft, send_sem=halo_send.at[0], recv_sem=halo_recv.at[0],
            device_id=(right,), device_id_type=MESH,
        ),
        pltpu.make_async_remote_copy(
            src_ref=vel.at[:, 0:3], dst_ref=vright, send_sem=halo_send.at[1], recv_sem=halo_recv.at[1],
            device_id=(left,), device_id_type=MESH,
        ),
    ]

    def start(j, carry):
        copy_to(partner(j, n)).start()
        return carry

    lax.fori_loop(0, n - 1, start, 0)
    for halo in halos:
        halo.start()

    def finish(i, carry):
        copy = pltpu.make_async_remote_copy(
            src_ref=send.at[lax.rem(me + i, n)], dst_ref=rec.at[lax.rem(me + n - i, n)],
            send_sem=send_sem.at[i], recv_sem=recv_sem.at[i], device_id=(right,), device_id_type=MESH,
        )
        copy.wait()
        return carry

    lax.fori_loop(1, n, finish, 0)
    for halo in halos:
        halo.wait()
    own.wait()


def fluid_kernel(
    n, cap, starts, vel, vleft, vright, fmid, rec, new, got,
    u0, u1, fext, u4, back, send_sem, recv_sem, halo_send, halo_recv,
):
    me = lax.axis_index("slab")
    right, left = lax.rem(me + 1, n), lax.rem(me + n - 1, n)
    planes, ny, nz = vel.shape[1], vel.shape[2], vel.shape[3]
    nodes = rec.shape[2]
    meet_all(n, me)
    halos = [
        pltpu.make_async_remote_copy(
            src_ref=fmid.at[planes - 2:], dst_ref=fext.at[0:2], send_sem=halo_send.at[0],
            recv_sem=halo_recv.at[0], device_id=(right,), device_id_type=MESH,
        ),
        pltpu.make_async_remote_copy(
            src_ref=fmid.at[0:2], dst_ref=fext.at[2 + planes:4 + planes], send_sem=halo_send.at[1],
            recv_sem=halo_recv.at[1], device_id=(left,), device_id_type=MESH,
        ),
    ]
    for halo in halos:
        halo.start()
    u0[:, 0:3] = vleft[...]
    u0[:, 3:3 + planes] = vel[...]
    u0[:, 3 + planes:6 + planes] = vright[...]
    lane = lax.broadcasted_iota(jnp.int32, (ny, nz), 1)

    def step(src, dst, first, last, force, shift):
        def plane(p, carry):
            packed = force[p - shift]
            center = [src[c, p] for c in range(3)]
            for c in range(3):
                mid = center[c]
                ahead = src[c, p + 1]
                behind = src[c, p - 1]
                y_plus = pltpu.roll(mid, ny - 1, 0)
                y_minus = pltpu.roll(mid, 1, 0)
                z_plus = pltpu.roll(mid, nz - 1, 1)
                z_minus = pltpu.roll(mid, 1, 1)
                push = packed if c == 0 else pltpu.roll(packed, nz - c * NZF, 1)
                push = jnp.where(lane < NZF, push, 0.0)
                laplace = ahead + behind + y_plus + y_minus + z_plus + z_minus - 6.0 * mid
                advect = (
                    center[0] * (ahead - behind)
                    + center[1] * (y_plus - y_minus)
                    + center[2] * (z_plus - z_minus)
                ) * 0.5
                dst[c, p] = mid + time_step * (viscosity * laplace - advect + push)
            return carry

        lax.fori_loop(first, last, plane, 0)

    step(u0, u1, 3, planes + 3, fmid, 3)
    for halo in halos:
        halo.wait()
    step(u0, u1, 1, 3, fext, 1)
    step(u0, u1, planes + 3, planes + 5, fext, 1)
    step(u1, u0, 2, 3, fext, 1)
    step(u1, u0, 3, planes + 3, fmid, 3)
    step(u1, u0, planes + 3, planes + 4, fext, 1)
    step(u0, u1, 3, planes + 3, fmid, 3)
    new[...] = u1[:, 3:3 + planes]

    for a in range(CX):
        for c in range(3):
            u = u1[c, 3 + a][:, 0:NZF]
            high = u.astype(jnp.bfloat16).astype(jnp.float32)
            low = u - high
            u4[c, :, a, :] = jnp.concatenate([high, low, high, low], axis=1)

    iota8 = lax.broadcasted_iota(jnp.int32, (TAPS, nodes), 0).astype(jnp.float32)
    iota32 = lax.broadcasted_iota(jnp.int32, (NZF, nodes), 0).astype(jnp.float32)

    def answer(s, put, place):
        for r in range(cap):
            start = starts[s * cap + r]
            joint = joint_weights(rec, s, r, cap, start, iota8)
            wh, wl = split(z_weights(rec, s, r, cap, iota32))
            window = jnp.concatenate(
                [u4[c, start + i] for c in range(3) for i in range(TAPS)], axis=0
            ).astype(jnp.bfloat16)
            part = jnp.dot(
                window, jnp.concatenate([wh, wh, wl, wl], axis=0), preferred_element_type=jnp.float32
            )
            for c in range(3):
                mine = part[c * TAPS * CX:(c + 1) * TAPS * CX] * joint
                put[place, c * cap + r:c * cap + r + 1, :] = jnp.sum(mine, axis=0, keepdims=True)

    def serve(j, carry):
        i = partner(j, n)
        s = lax.rem(me + i, n)
        answer(s, back, s)
        pltpu.make_async_remote_copy(
            src_ref=back.at[s], dst_ref=got.at[me], send_sem=send_sem.at[i], recv_sem=recv_sem.at[i],
            device_id=(s,), device_id_type=MESH,
        ).start()
        return carry

    lax.fori_loop(0, n - 1, serve, 0)
    answer(me, got, me)

    def finish(i, carry):
        pltpu.make_async_remote_copy(
            src_ref=back.at[lax.rem(me + i, n)], dst_ref=got.at[lax.rem(me + n - i, n)],
            send_sem=send_sem.at[i], recv_sem=recv_sem.at[i], device_id=(right,), device_id_type=MESH,
        ).wait()
        return carry

    lax.fori_loop(1, n, finish, 0)


def unpack_kernel(cap, slots, got, out):
    def one(k, carry):
        slot = slots[k]
        d = slot // cap
        r = slot - d * cap
        for c in range(3):
            out[c, pl.ds(k, 1), :] = got[d, pl.ds(c * cap + r, 1), :]
        return carry

    lax.fori_loop(0, out.shape[1], one, 0, unroll=4)


MESH = pl.DeviceIdType.MESH
VMEM = pl.BlockSpec(memory_space=pltpu.VMEM)
SMEM = pl.BlockSpec(memory_space=pltpu.SMEM)
PARAMS = pltpu.CompilerParams(vmem_limit_bytes=40 * 1024 * 1024)


def body(velocity, node_coords, node_force, block_slab, block_offset):
    devices = lax.axis_size("slab")
    blocks, _, nodes = node_coords.shape
    cap = 2 * blocks // devices
    _, planes, ny, nz = velocity.shape
    f32 = jnp.float32

    send, slots = pl.pallas_call(
        functools.partial(pack_kernel, cap),
        out_shape=(
            jax.ShapeDtypeStruct((devices, ROWS * cap, nodes), f32),
            jax.ShapeDtypeStruct((blocks,), jnp.int32),
        ),
        in_specs=[SMEM, SMEM, VMEM, VMEM],
        out_specs=(VMEM, SMEM),
        scratch_shapes=[pltpu.SMEM((devices,), jnp.int32)],
        compiler_params=PARAMS,
    )(block_slab.reshape(blocks), block_offset.reshape(2 * blocks), jnp.transpose(node_coords, (1, 0, 2)), jnp.transpose(node_force, (1, 0, 2)))

    halo = jax.ShapeDtypeStruct((3, 3, ny, nz), f32)
    rec, vleft, vright = pl.pallas_call(
        functools.partial(exchange_kernel, devices),
        out_shape=(jax.ShapeDtypeStruct(send.shape, f32), halo, halo),
        in_specs=[VMEM, VMEM],
        out_specs=(VMEM, VMEM, VMEM),
        scratch_shapes=[
            pltpu.SemaphoreType.DMA((devices,)),
            pltpu.SemaphoreType.DMA((devices,)),
            pltpu.SemaphoreType.DMA,
            pltpu.SemaphoreType.DMA((2,)),
            pltpu.SemaphoreType.DMA((2,)),
        ],
        compiler_params=pltpu.CompilerParams(
            vmem_limit_bytes=40 * 1024 * 1024, collective_id=0, has_side_effects=True
        ),
    )(send, velocity)
    first = rec[:, 6 * cap:, 0].astype(jnp.int32).reshape(devices * cap)
    starts = jnp.clip(first - 1, 0, ny - TAPS)

    fmid = pl.pallas_call(
        functools.partial(spread_kernel, cap, ny),
        out_shape=jax.ShapeDtypeStruct((planes, ny, nz), f32),
        in_specs=[SMEM, VMEM],
        out_specs=VMEM,
        scratch_shapes=[pltpu.VMEM((ny * CX, nz), f32)],
        compiler_params=PARAMS,
    )(starts, rec)

    new, got = pl.pallas_call(
        functools.partial(fluid_kernel, devices, cap),
        out_shape=(
            jax.ShapeDtypeStruct(velocity.shape, f32),
            jax.ShapeDtypeStruct((devices, 3 * cap, nodes), f32),
        ),
        in_specs=[SMEM] + [VMEM] * 5,
        out_specs=(VMEM, VMEM),
        scratch_shapes=[
            pltpu.VMEM((3, planes + 6, ny, nz), f32),
            pltpu.VMEM((3, planes + 6, ny, nz), f32),
            pltpu.VMEM((planes + 4, ny, nz), f32),
            pltpu.VMEM((3, ny, CX, nz), f32),
            pltpu.VMEM((devices, 3 * cap, nodes), f32),
            pltpu.SemaphoreType.DMA((devices,)),
            pltpu.SemaphoreType.DMA((devices,)),
            pltpu.SemaphoreType.DMA((2,)),
            pltpu.SemaphoreType.DMA((2,)),
        ],
        compiler_params=pltpu.CompilerParams(
            vmem_limit_bytes=40 * 1024 * 1024, collective_id=1, has_side_effects=True
        ),
    )(starts, velocity, vleft, vright, fmid, rec)

    node_velocity = pl.pallas_call(
        functools.partial(unpack_kernel, cap),
        out_shape=jax.ShapeDtypeStruct((3, blocks, nodes), f32),
        in_specs=[SMEM, VMEM],
        out_specs=VMEM,
        compiler_params=PARAMS,
    )(slots, got)
    return new, jnp.transpose(node_velocity, (1, 0, 2))


def solution(mesh):
    return jax.shard_map(
        body,
        mesh=mesh,
        in_specs=(
            P(None, "slab", None, None),
            P("slab", None, None),
            P("slab", None, None),
            P("slab", None),
            P("slab", None),
        ),
        out_specs=(P(None, "slab", None, None), P("slab", None, None)),
        check_vma=False,
    )
```
